256 devices in a mesh: row: 64 (over z, x_hi, y), head: 4 (over x_lo, core).
Axes of the slice: x: 4 (x_hi: 2, x_lo: 2; x = x_hi * 2 + x_lo), y: 4, z: 8, core: 2. Of those that a mesh axis runs over, the one named last changes fastest.
Arguments:
- samples: bfloat16 [128, 512, 2048], P('row', None, 'head'), may hold values from -12 to 12
- norm_gain: float32 [2048], replicated, may hold values from 0.25 to 1.75
- row_qkv: bfloat16 [3, 2048, 1024], P(None, None, 'head'), may hold values from -0.09082975 to 0.09082975
- col_qkv: bfloat16 [3, 2048, 1024], P(None, None, 'head'), may hold values from -0.09082975 to 0.09082975
- row_out: bfloat16 [1024, 2048], P('head'), may hold values from -0.1875 to 0.1875
- col_out: bfloat16 [1024, 2048], P('head'), may hold values from -0.1875 to 0.1875
Outputs:
- layer_out: bfloat16 [128, 512, 2048], P('row', None, 'head')
The draws below stay inside these ranges and needn't reach their ends.
All inputs are finite; a program needn't handle non-finite values.
Results may differ from the reference program's by a relative error of at most 0.012.
Values may be sent and summed in bfloat16 or wider, within the bound.
No kernel may reach another device: no remote copies, remote signals or barrier semaphores. Data moves between devices by JAX's collectives and lax.ppermute only.
A program may use at most 64 MiB of HBM per device.

```python
import jax
import jax.numpy as jnp
from jax import lax

D = 2048
HD = 128
RHEADS = 8
CHEADS = 8
COLS = 512
ROWS = 128


def draw_samples(key, part):
    own_key = jax.random.fold_in(key, 3)
    gaussian = jnp.clip(jax.random.normal(own_key, (ROWS, COLS, D), jnp.float32), -6.0, 6.0)
    return gaussian.astype(jnp.bfloat16)


def draw_row_qkv(key, part):
    own_key = jax.random.fold_in(key, 5)
    weights = jnp.clip(jax.random.normal(own_key, (3, D, RHEADS * HD), jnp.float32), -3.98, 3.98) * D ** (-0.5)
    return weights.astype(jnp.bfloat16)


def draw_col_qkv(key, part):
    own_key = jax.random.fold_in(key, 7)
    weights = jnp.clip(jax.random.normal(own_key, (3, D, CHEADS * HD), jnp.float32), -3.98, 3.98) * D ** (-0.5)
    return weights.astype(jnp.bfloat16)


def strengthened(drawn, key, source, target, blocks, factor):
    def block_of(position):
        return (jnp.arange(drawn.shape[position]) // (drawn.shape[position] // blocks)).reshape((-1,) + (1,) * (drawn.ndim - 1 - position))

    one_side = jax.random.permutation(key, blocks)[block_of(target)]
    other_side = (block_of(target) + blocks // 2) % blocks
    return jnp.where((block_of(source) == one_side) | (block_of(source) == other_side), factor * drawn, drawn)


def block_scale(stream_key, extent, shards, smallest, top_value):
    loudness = 1.0
    for dim, shards_of in shards:
        heights = jax.random.uniform(jax.random.fold_in(jax.random.fold_in(stream_key, 6), dim), (shards_of,), jnp.float32, smallest / len(shards), top_value / len(shards))
        loudness = loudness * jnp.repeat(jnp.exp(heights), extent[dim] // shards_of).reshape((-1,) + (1,) * (len(extent) - 1 - dim))
    return loudness


def bell_draw_with(stream_key, shape, deviation, bound, split, heavy, kind=jnp.bfloat16):
    drawn = deviation * jax.random.normal(stream_key, shape, jnp.float32)
    if split:
        drawn = drawn * block_scale(stream_key, shape, split, -0.22, 0.18)
    return jnp.clip(strengthened(drawn, jax.random.fold_in(stream_key, 3), *heavy), -bound, bound).astype(kind)


def setup_inputs(seed: int = 0) -> dict:
    arg_keys = jax.random.split(jax.random.key(seed), 7)
    samples = draw_samples(jax.random.fold_in(arg_keys[6], 71), 0)
    norm_gain = jnp.clip(1.0 + 0.15 * jax.random.normal(arg_keys[1], (D,), jnp.float32), 0.25, 1.75)
    row_qkv = draw_row_qkv(jax.random.fold_in(arg_keys[6], 71), 0)
    col_qkv = draw_col_qkv(jax.random.fold_in(arg_keys[6], 71), 0)
    row_out = bell_draw_with(arg_keys[4], (RHEADS * HD, D), ((RHEADS + CHEADS) * HD) ** -0.5, 0.1875, ((0, 4),), (0, 1, 4, 2.0))
    col_out = bell_draw_with(arg_keys[5], (CHEADS * HD, D), ((RHEADS + CHEADS) * HD) ** -0.5, 0.1875, ((0, 4),), (0, 1, 4, 2.0))
    return {"samples": samples, "norm_gain": norm_gain, "row_qkv": row_qkv, "col_qkv": col_qkv, "row_out": row_out, "col_out": col_out}


def layer_norm(values, norm_gain):
    values = values.astype(jnp.float32)
    mean = lax.optimization_barrier(jnp.mean(values, axis=-1, keepdims=True))
    centred = values - mean
    var = lax.optimization_barrier(jnp.mean(centred * centred, axis=-1, keepdims=True))
    return (centred * lax.rsqrt(var + 1e-05) * norm_gain).astype(jnp.bfloat16)

def softmax_rounded(scores, allowed):
    scores = jnp.where(allowed, scores, -jnp.inf)
    top = lax.optimization_barrier(jnp.max(scores, axis=-1, keepdims=True))
    expo = jnp.exp(scores - top)
    return (expo / lax.optimization_barrier(jnp.sum(expo, axis=-1, keepdims=True))).astype(jnp.bfloat16)

def reference(samples, norm_gain, row_qkv, col_qkv, row_out, col_out):
    scale = 1.0 / HD ** 0.5
    normed = layer_norm(samples, norm_gain).reshape(ROWS * COLS, D)
    row_parts = [jnp.dot(normed, row_qkv[t], preferred_element_type=jnp.float32).astype(jnp.bfloat16) for t in range(3)]
    col_parts = [jnp.dot(normed, col_qkv[t], preferred_element_type=jnp.float32).astype(jnp.bfloat16) for t in range(3)]
    row_stack = jnp.stack(row_parts).reshape(3, ROWS, COLS, RHEADS, HD)
    col_stack = jnp.stack(col_parts).reshape(3, ROWS, COLS, CHEADS, HD)
    causal_cols = jnp.arange(COLS)[:, None] >= jnp.arange(COLS)[None, :]

    def one_row(parts):
        query, keys, vals = (parts[0].astype(jnp.float32), parts[1].astype(jnp.float32), parts[2].astype(jnp.float32))
        scores = jnp.einsum('qhe,khe->hqk', query, keys) * scale
        weights = softmax_rounded(scores, causal_cols[None])
        return jnp.einsum('hqk,khe->qhe', weights.astype(jnp.float32), vals).astype(jnp.bfloat16)
    row_attn = lax.map(one_row, jnp.transpose(row_stack, (1, 0, 2, 3, 4)))
    causal_rows = jnp.arange(ROWS)[:, None] >= jnp.arange(ROWS)[None, :]

    def one_head(parts):
        query, keys, vals = (parts[0].astype(jnp.float32), parts[1].astype(jnp.float32), parts[2].astype(jnp.float32))
        scores = jnp.einsum('qce,kce->cqk', query, keys) * scale
        weights = softmax_rounded(scores, causal_rows[None])
        return jnp.einsum('cqk,kce->qce', weights.astype(jnp.float32), vals).astype(jnp.bfloat16)
    col_attn = lax.map(one_head, jnp.transpose(col_stack, (3, 0, 1, 2, 4)))
    col_attn = jnp.transpose(col_attn, (1, 2, 0, 3))
    projected = jnp.dot(row_attn.reshape(ROWS * COLS, RHEADS * HD), row_out, preferred_element_type=jnp.float32)
    projected = projected + jnp.dot(col_attn.reshape(ROWS * COLS, CHEADS * HD), col_out, preferred_element_type=jnp.float32)
    total = samples.astype(jnp.float32) + projected.reshape(ROWS, COLS, D)
    return total.astype(jnp.bfloat16)
```

```python
import math

import jax
import jax.numpy as jnp
from jax import lax
from jax.experimental import pallas as pl
from jax.experimental.pallas import tpu as pltpu
from jax.sharding import PartitionSpec as P

HD = 128
CHUNKS = 2
OWNED = 4
F32 = jnp.float32
BF16 = jnp.bfloat16
MIB = 2**20
VM = pl.BlockSpec(memory_space=pltpu.VMEM)
SM = pl.BlockSpec(memory_space=pltpu.SMEM)


def call(body, ins, outs, flops, scratch=(), scalars=1):
    moved = sum(math.prod(x.shape) * x.dtype.itemsize for x in list(ins) + list(outs))
    return pl.pallas_call(
        body,
        out_shape=tuple(outs),
        in_specs=[SM] * scalars + [VM] * (len(ins) - scalars),
        out_specs=tuple([VM] * len(outs)),
        scratch_shapes=list(scratch),
        compiler_params=pltpu.CompilerParams(vmem_limit_bytes=28 * MIB),
        cost_estimate=pl.CostEstimate(flops=flops, bytes_accessed=moved, transcendentals=0),
    )(*ins)


def sds(shape, dtype=BF16):
    return jax.ShapeDtypeStruct(shape, dtype)


def block(number, width):
    return pl.ds(pl.multiple_of(number * width, width), width)


def interleave(first, second):
    n, f = first.shape
    a, b = first.reshape(n // 8, 8, f), second.reshape(n // 8, 8, f)
    low = lax.broadcasted_iota(jnp.int32, a.shape, 1) < OWNED
    t0 = jnp.where(low, a, pltpu.roll(b, OWNED, 1))
    t1 = jnp.where(low, pltpu.roll(a, OWNED, 1), b)
    return jnp.stack([t0, t1], axis=1).reshape(2 * n, f)


def deinterleave(tokens):
    n, f = tokens.shape
    both = tokens.reshape(n // 16, 2, 8, f)
    t0, t1 = both[:, 0], both[:, 1]
    low = lax.broadcasted_iota(jnp.int32, t0.shape, 1) < OWNED
    a = jnp.where(low, t0, pltpu.roll(t1, OWNED, 1))
    b = jnp.where(low, pltpu.roll(t0, OWNED, 1), t1)
    return a.reshape(n // 2, f), b.reshape(n // 2, f)


def norm_project_kernel(h_ref, a_ref, b_ref, c_ref, d_ref, gain_ref, w_ref, normed_ref, qkv_ref):
    h = h_ref[0]
    parts = ((a_ref, 0), (b_ref, 2), (c_ref, 1), (d_ref, 3))
    _, cols, width = a_ref.shape
    features = 4 * width
    tile = min(32, cols)

    @pl.loop(0, cols // tile)
    def _(i):
        at = pl.ds(pl.multiple_of(i * tile, tile), tile)
        stats = []
        for r in range(2):
            total = sum(jnp.sum(ref[r, at, :].astype(F32), axis=-1, keepdims=True) for ref, _ in parts)
            mean = total * (1.0 / features)
            sq = 0.0
            for ref, _ in parts:
                centred = ref[r, at, :].astype(F32) - mean
                sq = sq + jnp.sum(centred * centred, axis=-1, keepdims=True)
            stats.append((mean, lax.rsqrt(sq * (1.0 / features) + 1e-05)))
        for ref, flip in parts:
            where = block(h ^ flip, width)
            gain = gain_ref[:, where]
            rows = [(ref[r, at, :].astype(F32) - stats[r][0]) * stats[r][1] * gain for r in range(2)]
            to = pl.ds(pl.multiple_of(i * 2 * tile, 2 * tile), 2 * tile)
            normed_ref[to, where] = interleave(*rows).astype(BF16)

    for t in range(3):
        wide = w_ref.shape[2]
        qkv_ref[:, t * wide : (t + 1) * wide] = jnp.dot(
            normed_ref[...], w_ref[t], preferred_element_type=F32
        ).astype(BF16)


def attend(q_ref, q_at, keys, vals, start, bits, out_ref, out_at):
    n = q_ref.shape[0]
    tile = min(256, n)
    factor = math.log2(math.e) / HD**0.5
    for i in range(n // tile):
        q = q_ref[i * tile : (i + 1) * tile, q_at]
        scores = []
        upto = start + (i + 1) * tile
        used = []
        base = 0
        for k_ref, k_at in keys:
            have = k_ref.shape[0]
            take = min(have, upto - base)
            used.append((base, take))
            s = lax.dot_general(q, k_ref[:take, k_at], (((1,), (1,)), ((), ())), preferred_element_type=F32)
            ta = lax.broadcasted_iota(jnp.int32, s.shape, 0) + (start + i * tile)
            tb = lax.broadcasted_iota(jnp.int32, s.shape, 1) + base
            ok = (((ta ^ tb) & bits) == 0) & (tb <= ta)
            scores.append(jnp.where(ok, s * factor, -jnp.inf))
            base += have
        top = scores[0].max(axis=-1, keepdims=True)
        for s in scores[1:]:
            top = jnp.maximum(top, s.max(axis=-1, keepdims=True))
        expo = [jnp.exp2(s - top) for s in scores]
        total = sum(e.sum(axis=-1, keepdims=True) for e in expo)
        out = 0.0
        for e, (v_ref, v_at), (_, take) in zip(expo, vals, used):
            out = out + jnp.dot(e.astype(BF16), v_ref[:take, v_at], preferred_element_type=F32)
        out_ref[i * tile : (i + 1) * tile, out_at] = (out / total).astype(BF16)


def lanes(t, head, wide):
    return slice(t * wide + head * HD, t * wide + (head + 1) * HD)


def row_kernel(*refs):
    normed_ref, w_ref = refs[:2]
    earlier = refs[2:-2]
    attn_ref, qkv_ref = refs[-2:]
    wide = w_ref.shape[2]
    for t in range(3):
        qkv_ref[:, t * wide : (t + 1) * wide] = jnp.dot(
            normed_ref[...], w_ref[t], preferred_element_type=F32
        ).astype(BF16)
    sources = list(earlier) + [qkv_ref]
    start = sum(e.shape[0] for e in earlier)
    for head in range(wide // HD):
        attend(
            qkv_ref,
            lanes(0, head, wide),
            [(s, lanes(1, head, wide)) for s in sources],
            [(s, lanes(2, head, wide)) for s in sources],
            start,
            OWNED,
            attn_ref,
            lanes(0, head, wide),
        )


def col_kernel(qkv_ref, attn_ref):
    wide = attn_ref.shape[1]
    for head in range(wide // HD):
        attend(
            qkv_ref,
            lanes(0, head, wide),
            [(qkv_ref, lanes(1, head, wide))],
            [(qkv_ref, lanes(2, head, wide))],
            0,
            OWNED - 1,
            attn_ref,
            lanes(0, head, wide),
        )


def out_dot(row_ref, col_ref, wr_ref, wc_ref, where):
    return jnp.dot(row_ref[...], wr_ref[:, where], preferred_element_type=F32) + jnp.dot(
        col_ref[...], wc_ref[:, where], preferred_element_type=F32
    )


def out_core_kernel(h_ref, row_ref, col_ref, wr_ref, wc_ref, y3_ref, y1_ref):
    h = h_ref[0]
    width = y3_ref.shape[1]
    y3_ref[...] = out_dot(row_ref, col_ref, wr_ref, wc_ref, block(h ^ 3, width)).astype(BF16)
    y1_ref[...] = out_dot(row_ref, col_ref, wr_ref, wc_ref, block(h ^ 1, width)).astype(BF16)


def out_chip_kernel(h_ref, row_ref, col_ref, wr_ref, wc_ref, r2_ref, s2_ref):
    width = s2_ref.shape[1]
    own = out_dot(row_ref, col_ref, wr_ref, wc_ref, block(h_ref[0] ^ 2, width))
    s2_ref[...] = (own + r2_ref[...].astype(F32)).astype(BF16)


def out_own_kernel(h_ref, row_ref, col_ref, wr_ref, wc_ref, r0_ref, own_ref):
    width = own_ref.shape[1]
    own = out_dot(row_ref, col_ref, wr_ref, wc_ref, block(h_ref[0], width))
    own_ref[...] = own + r0_ref[...].astype(F32)


def final_kernel(samples_ref, *refs):
    out_ref = refs[-1]
    cols = samples_ref.shape[1] // CHUNKS
    for k in range(CHUNKS):
        own_ref, rx_ref = refs[2 * k], refs[2 * k + 1]
        step = min(64, cols)

        @pl.loop(0, cols // step)
        def _(i):
            tok = pl.ds(pl.multiple_of(i * 2 * step, 2 * step), 2 * step)
            pair = deinterleave(own_ref[tok, :] + rx_ref[tok, :].astype(F32))
            at = pl.ds(pl.multiple_of(k * cols + i * step, step), step)
            for r in range(2):
                out_ref[r, at, :] = (samples_ref[r, at, :].astype(F32) + pair[r]).astype(BF16)


def shards(samples, norm_gain, row_qkv, col_qkv, row_out, col_out):
    rows, cols, width = samples.shape
    wide = col_qkv.shape[2]
    features = 4 * width
    part = cols // CHUNKS
    tokens = rows * part
    h = lax.axis_index("head").astype(jnp.int32).reshape(1)
    gain = norm_gain.reshape(1, features)

    def over_chip(x):
        return lax.ppermute(x, "head", [(i, i ^ 2) for i in range(4)])

    def over_core(x):
        return lax.ppermute(x, "head", [(i, i ^ 1) for i in range(4)])

    def exchange(x):
        return lax.all_to_all(x, "row", 0, 0, tiled=True)

    qkv_flops = 2 * tokens * features * 3 * wide
    moved, normed = [], []
    for k in range(CHUNKS):
        a = samples[:, k * part : (k + 1) * part, :]
        b = over_chip(a)
        c = over_core(a)
        d = over_core(b)
        n, col = call(
            norm_project_kernel,
            (h, a, b, c, d, gain, col_qkv),
            (sds((tokens, features)), sds((tokens, 3 * wide))),
            qkv_flops,
        )
        normed.append(n)
        moved.append(exchange(col))
    row_attn, row_state = [], []
    for k in range(CHUNKS):
        attn, state = call(
            row_kernel,
            (normed[k], row_qkv, *row_state),
            (sds((tokens, wide)), sds((tokens, 3 * wide))),
            qkv_flops + 4 * (k + 1) * tokens * tokens * wide,
            scalars=0,
        )
        row_attn.append(attn)
        row_state.append(state)
    pairs = []
    for k in range(CHUNKS):
        (attn,) = call(
            col_kernel, (moved[k],), (sds((tokens, wide)),), 4 * tokens * tokens * wide, scalars=0
        )
        ops = (h, row_attn[k], exchange(attn), row_out, col_out)
        piece = 4 * tokens * wide * width
        y3, y1 = call(out_core_kernel, ops, (sds((tokens, width)),) * 2, 2 * piece)
        (s2,) = call(out_chip_kernel, ops + (over_core(y3),), (sds((tokens, width)),), piece)
        (own,) = call(out_own_kernel, ops + (over_core(y1),), (sds((tokens, width), F32),), piece)
        pairs += [own, over_chip(s2)]
    (out,) = call(final_kernel, (samples, *pairs), (sds(samples.shape),), samples.size, scalars=0)
    return out


def solution(mesh):
    placed = (
        P("row", None, "head"),
        P(),
        P(None, None, "head"),
        P(None, None, "head"),
        P("head", None),
        P("head", None),
    )
    return jax.shard_map(
        shards, mesh=mesh, in_specs=placed, out_specs=P("row", None, "head"), check_vma=False
    )
```

```python
import functools
import math

import jax
import jax.numpy as jnp
from jax import lax
from jax.experimental import pallas as pl
from jax.experimental.pallas import tpu as pltpu
from jax.sharding import PartitionSpec as P

HD = 128
OWNED = 4
F32 = jnp.float32
BF16 = jnp.bfloat16
ROOMY, WHOLE = 24, 60
SM = pl.BlockSpec(memory_space=pltpu.SMEM)
ANY = pl.BlockSpec(memory_space=pl.ANY)


VM = pl.BlockSpec(memory_space=pltpu.VMEM)


def params(limit):
    return pltpu.CompilerParams(vmem_limit_bytes=limit * 2**20)


def cost(flops, arrays, weight=1):
    moved = sum(math.prod(x.shape) * x.dtype.itemsize for x in arrays)
    return pl.CostEstimate(flops=flops * weight, bytes_accessed=moved * weight, transcendentals=0)


def call(body, scalars, ins, raws, outs, flops, scratch=(), after=()):
    used = len(scalars) + len(ins) + len(raws)

    def kernel(*refs):
        body(*refs[:used], *refs[used + len(after) :])

    return pl.pallas_call(
        kernel,
        out_shape=tuple(outs),
        in_specs=[SM] * len(scalars) + [VM] * len(ins) + [ANY] * (len(raws) + len(after)),
        out_specs=tuple([VM] * len(outs)),
        scratch_shapes=list(scratch),
        compiler_params=params(ROOMY),
        cost_estimate=cost(flops, list(ins) + list(raws) + list(outs)),
    )(*scalars, *ins, *raws, *after)


def sds(shape, dtype=BF16):
    return jax.ShapeDtypeStruct(shape, dtype)


def block(number, width):
    return pl.ds(pl.multiple_of(number * width, width), width)


def interleave(first, second):
    n, f = first.shape
    a, b = first.reshape(n // 8, 8, f), second.reshape(n // 8, 8, f)
    low = lax.broadcasted_iota(jnp.int32, a.shape, 1) < OWNED
    t0 = jnp.where(low, a, pltpu.roll(b, OWNED, 1))
    t1 = jnp.where(low, pltpu.roll(a, OWNED, 1), b)
    return t0.reshape(n, f), t1.reshape(n, f)


def deinterleave(t0, t1):
    n, f = t0.shape
    t0, t1 = t0.reshape(n // 8, 8, f), t1.reshape(n // 8, 8, f)
    low = lax.broadcasted_iota(jnp.int32, t0.shape, 1) < OWNED
    a = jnp.where(low, t0, pltpu.roll(t1, OWNED, 1))
    b = jnp.where(low, pltpu.roll(t0, OWNED, 1), t1)
    return a.reshape(n, f), b.reshape(n, f)


def fetch(sources, targets, sems):
    copies = [pltpu.make_async_copy(s, t, sems.at[i]) for i, (s, t) in enumerate(zip(sources, targets))]
    for copy in copies:
        copy.start()
    return copies


def lanes(t, head, wide):
    return slice(t * wide + head * HD, t * wide + (head + 1) * HD)


def attend(q_ref, q_at, keys, vals, start, bits, out_ref, out_at):
    n = q_ref.shape[0]
    tile = min(256, n)
    factor = math.log2(math.e) / HD**0.5
    for i in range(n // tile):
        q = q_ref[i * tile : (i + 1) * tile, q_at]
        scores = []
        upto = start + (i + 1) * tile
        used = []
        base = 0
        for k_ref, k_at in keys:
            have = k_ref.shape[0]
            take = min(have, upto - base)
            used.append((base, take))
            s = lax.dot_general(q, k_ref[:take, k_at], (((1,), (1,)), ((), ())), preferred_element_type=F32)
            ta = lax.broadcasted_iota(jnp.int32, s.shape, 0) + (start + i * tile)
            tb = lax.broadcasted_iota(jnp.int32, s.shape, 1) + base
            ok = (((ta ^ tb) & bits) == 0) & (tb <= ta)
            scores.append(jnp.where(ok, s * factor, -jnp.inf))
            base += have
        top = scores[0].max(axis=-1, keepdims=True)
        for s in scores[1:]:
            top = jnp.maximum(top, s.max(axis=-1, keepdims=True))
        expo = [jnp.exp2(s - top) for s in scores]
        total = sum(e.sum(axis=-1, keepdims=True) for e in expo)
        out = 0.0
        for e, (v_ref, v_at), (_, take) in zip(expo, vals, used):
            out = out + jnp.dot(e.astype(BF16), v_ref[:take, v_at], preferred_element_type=F32)
        out_ref[i * tile : (i + 1) * tile, out_at] = (out / total).astype(BF16)


def permute_kernel(samples_hbm, out_hbm, in_ref, out_ref, sems):
    cols, width = samples_hbm.shape[1:]
    step = cols // 4
    spans = [pl.ds(i * step, step) for i in range(4)]
    arriving = fetch([samples_hbm.at[:, at] for at in spans], [in_ref.at[:, at] for at in spans], sems.at[0])
    leaving = []
    for i, at in enumerate(spans):
        arriving[i].wait()
        halves = interleave(in_ref[0, at, :].astype(F32), in_ref[1, at, :].astype(F32))
        tiles = jnp.stack([t.reshape(step // 8, 8, width) for t in halves], axis=1)
        to = pl.ds(i * 2 * step, 2 * step)
        out_ref[to, :] = tiles.reshape(2 * step, width).astype(BF16)
        leaving += fetch([out_ref.at[to]], [out_hbm.at[to]], sems.at[1, i : i + 1])
    for copy in leaving:
        copy.wait()


def permute(samples):
    rows, cols, width = samples.shape
    out = sds((rows * cols, width))
    return pl.pallas_call(
        permute_kernel,
        out_shape=out,
        in_specs=[ANY],
        out_specs=ANY,
        scratch_shapes=[
            pltpu.VMEM(samples.shape, BF16),
            pltpu.VMEM(out.shape, BF16),
            pltpu.SemaphoreType.DMA((2, 4)),
        ],
        compiler_params=params(WHOLE),
        cost_estimate=cost(samples.size, [samples, out]),
    )(samples)


def norm_into(h, refs, gain_ref, normed_ref):
    tokens, width = refs[0].shape
    features = 4 * width
    tile = min(32, tokens)

    @pl.loop(0, tokens // tile, unroll=2)
    def _(i):
        at = pl.ds(pl.multiple_of(i * tile, tile), tile)
        total = sum(ref[at, :].astype(F32) for ref in refs)
        mean = jnp.sum(total, axis=-1, keepdims=True) * (1.0 / features)
        squares = 0.0
        for ref in refs:
            centred = ref[at, :].astype(F32) - mean
            squares = squares + centred * centred
        var = jnp.sum(squares, axis=-1, keepdims=True) * (1.0 / features)
        scale = lax.rsqrt(var + 1e-05)
        for ref, flip in zip(refs, (0, 2, 1, 3)):
            where = block(h ^ flip, width)
            rows = (ref[at, :].astype(F32) - mean) * scale * gain_ref[:, where]
            normed_ref[at, where] = rows.astype(BF16)


def project(normed_ref, w_ref, copies, qkv_ref):
    wide = w_ref.shape[2]
    for t in range(3):
        copies[t].wait()
        qkv_ref[:, t * wide : (t + 1) * wide] = jnp.dot(
            normed_ref[...], w_ref[t], preferred_element_type=F32
        ).astype(BF16)


def heads(qkv_ref, bits, attn_ref):
    wide = attn_ref.shape[1]
    for head in range(wide // HD):
        keys, vals = lanes(1, head, wide), lanes(2, head, wide)
        attend(qkv_ref, lanes(0, head, wide), [(qkv_ref, keys)], [(qkv_ref, vals)], 0, bits, attn_ref, lanes(0, head, wide))


def fetch_weights(gain_hbm, w_hbm, gain_ref, w_ref, sems):
    return fetch([gain_hbm] + [w_hbm.at[t] for t in range(3)], [gain_ref] + [w_ref.at[t] for t in range(3)], sems)


def attention(h, parts, copies, bits, attn_ref, gain_ref, w_ref, normed_ref, qkv_ref):
    copies[0].wait()
    norm_into(h, parts, gain_ref, normed_ref)
    project(normed_ref, w_ref, copies[1:], qkv_ref)
    heads(qkv_ref, bits, attn_ref)


def attention_scratch(gain, weights, tokens):
    _, features, wide = weights.shape
    return [
        pltpu.VMEM(gain.shape, F32),
        pltpu.VMEM(weights.shape, BF16),
        pltpu.VMEM((tokens, features), BF16),
        pltpu.VMEM((tokens, 3 * wide), BF16),
    ]


def col_kernel(h_ref, a, b, c, d, gain_hbm, w_hbm, attn_ref, gain_ref, w_ref, normed_ref, qkv_ref, sems):
    copies = fetch_weights(gain_hbm, w_hbm, gain_ref, w_ref, sems)
    attention(h_ref[0], (a, b, c, d), copies, OWNED - 1, attn_ref, gain_ref, w_ref, normed_ref, qkv_ref)


def row_kernel(row, n_more, h_ref, *refs):
    parts_hbm, more_hbm, (gain_hbm, w_hbm) = refs[:4], refs[4 : 4 + n_more], refs[4 + n_more : 6 + n_more]
    rest = refs[6 + n_more + n_more :] if n_more else refs[6:]
    n_out = 2 if n_more else 1
    outs_hbm = rest[:n_out]
    x_ref, held_ref, gain_ref, w_ref, normed_ref, qkv_ref, sems, more_sems = rest[n_out:]
    ready = fetch([p.at[row] for p in parts_hbm], [x_ref.at[i] for i in range(4)], sems)
    copies = fetch_weights(gain_hbm, w_hbm, gain_ref, w_ref, sems.at[4:])
    earlier = fetch(more_hbm, [held_ref.at[0]], more_sems)
    for copy in ready:
        copy.wait()
    parts = [x_ref.at[i] for i in range(4)]
    attention(h_ref[0], parts, copies, 0, held_ref.at[n_more], gain_ref, w_ref, normed_ref, qkv_ref)
    if n_more:
        earlier[0].wait()
        halves = interleave(held_ref[0].astype(F32), held_ref[1].astype(F32))
        for i, half in enumerate(halves):
            held_ref[i] = half.astype(BF16)
    for copy in fetch([held_ref.at[i] for i in range(n_out)], outs_hbm, more_sems):
        copy.wait()


def out_dot(row_ref, col_ref, wr_ref, wc_ref, where):
    return jnp.dot(row_ref[...], wr_ref[:, where], preferred_element_type=F32) + jnp.dot(
        col_ref[...], wc_ref[:, where], preferred_element_type=F32
    )


def out_core_kernel(h_ref, row_ref, col_ref, wr_ref, wc_ref, y3_ref, y1_ref):
    h = h_ref[0]
    width = y3_ref.shape[1]
    y3_ref[...] = out_dot(row_ref, col_ref, wr_ref, wc_ref, block(h ^ 3, width)).astype(BF16)
    y1_ref[...] = out_dot(row_ref, col_ref, wr_ref, wc_ref, block(h ^ 1, width)).astype(BF16)


def out_chip_kernel(h_ref, row_ref, col_ref, wr_ref, wc_ref, r2_ref, s2_ref):
    width = s2_ref.shape[1]
    own = out_dot(row_ref, col_ref, wr_ref, wc_ref, block(h_ref[0] ^ 2, width))
    s2_ref[...] = (own + r2_ref[...].astype(F32)).astype(BF16)


def out_own_kernel(h_ref, row_ref, col_ref, wr_ref, wc_ref, r0_ref, own_ref):
    width = own_ref.shape[1]
    own = out_dot(row_ref, col_ref, wr_ref, wc_ref, block(h_ref[0], width))
    own_ref[...] = own + r0_ref[...].astype(F32)


def final_kernel(samples_ref, own0_ref, rx0_ref, own1_ref, rx1_ref, out_ref):
    cols = samples_ref.shape[1]
    step = min(64, cols)

    @pl.loop(0, cols // step)
    def _(i):
        at = pl.ds(pl.multiple_of(i * step, step), step)
        pair = deinterleave(
            own0_ref[at, :] + rx0_ref[at, :].astype(F32), own1_ref[at, :] + rx1_ref[at, :].astype(F32)
        )
        for r in range(2):
            out_ref[r, at, :] = (samples_ref[r, at, :].astype(F32) + pair[r]).astype(BF16)


def shards(samples, norm_gain, row_qkv, col_qkv, row_out, col_out):
    rows, cols, width = samples.shape
    assert rows == 2
    wide = col_qkv.shape[2]
    features = 4 * width
    tokens = cols
    h = lax.axis_index("head").astype(jnp.int32).reshape(1)
    gain = norm_gain.reshape(1, features)
    dma = pltpu.SemaphoreType.DMA

    def over_chip(x):
        return lax.ppermute(x, "head", [(i, i ^ 2) for i in range(4)])

    def over_core(x):
        return lax.ppermute(x, "head", [(i, i ^ 1) for i in range(4)])

    def exchange(x):
        return lax.all_to_all(x, "row", 0, 0, tiled=True)

    def gather(a):
        b = over_chip(a)
        return a, b, over_core(a), over_core(b)

    flops = 2 * tokens * features * 3 * wide + 4 * tokens * tokens * wide

    def cols(parts, after):
        return call(
            col_kernel,
            (h,),
            parts,
            (gain, col_qkv),
            (sds((tokens, wide)),),
            flops,
            attention_scratch(gain, col_qkv, tokens) + [dma((4,))],
            after,
        )[0]

    def row(r, parts, more, after):
        outs = tuple([sds((tokens, wide))] * (1 + len(more)))
        return pl.pallas_call(
            functools.partial(row_kernel, r, len(more)),
            out_shape=outs,
            in_specs=[SM] + [ANY] * (6 + len(more) + len(after)),
            out_specs=tuple([ANY] * len(outs)),
            scratch_shapes=[pltpu.VMEM((4, tokens, width), BF16), pltpu.VMEM((2, tokens, wide), BF16)]
            + attention_scratch(gain, row_qkv, tokens)
            + [dma((8,)), dma((2,))],
            compiler_params=params(WHOLE),
            cost_estimate=cost(flops, parts, 4),
        )(h, *parts, *more, gain, row_qkv, *after)

    piece = 4 * tokens * wide * width

    def out(row_attn, col_attn, after, after_chip):
        ops = (row_attn, col_attn, row_out, col_out)
        y3, y1 = call(out_core_kernel, (h,), ops, (), (sds((tokens, width)),) * 2, 2 * piece, (), after)
        (s2,) = call(out_chip_kernel, (h,), ops + (over_core(y3),), (), (sds((tokens, width)),), piece, (), after_chip)

        def own(after):
            more = ops + (over_core(y1),)
            return call(out_own_kernel, (h,), more, (), (sds((tokens, width), F32),), piece, (), after)[0]

        return own, s2, over_chip(s2)

    every = gather(samples)
    mine = exchange(permute(samples)).reshape(-1, 2, 2 * OWNED, width)
    (row0,) = row(0, every, (), ())
    mine, row0 = lax.optimization_barrier((mine, row0))
    start0 = mine[:, 0].reshape(tokens, width)
    chip0 = over_chip(start0)
    mine, _ = lax.optimization_barrier((mine, chip0))
    start1 = mine[:, 1].reshape(tokens, width)
    chip1 = over_chip(start1)
    rows0, rows1 = row(1, every, (row0,), (row0,))
    chip0, rows0 = lax.optimization_barrier((chip0, rows0))
    parts0 = (start0, chip0, over_core(start0), over_core(chip0))
    attn0 = cols(parts0, (rows0,))
    back0 = exchange(attn0)
    start1, chip1, _ = lax.optimization_barrier((start1, chip1, attn0))
    attn1 = cols((start1, chip1, over_core(start1), over_core(chip1)), (attn0,))
    back1 = exchange(attn1)
    own0, s0, rx0 = out(rows0, back0, (attn1,), ())
    own1, s1, rx1 = out(rows1, back1, (s0,), (rx0,))
    own0 = own0((s1,))
    own1 = own1((own0,))
    return call(final_kernel, (), (samples, own0, rx0, own1, rx1), (), (sds(samples.shape),), samples.size)[0]


def solution(mesh):
    placed = (
        P("row", None, "head"),
        P(),
        P(None, None, "head"),
        P(None, None, "head"),
        P("head", None),
        P("head", None),
    )
    return jax.shard_map(
        shards, mesh=mesh, in_specs=placed, out_specs=P("row", None, "head"), check_vma=False
    )
```

```python
import functools
import math

import jax
import jax.numpy as jnp
from jax import lax
from jax.experimental import pallas as pl
from jax.experimental.pallas import tpu as pltpu
from jax.sharding import PartitionSpec as P

HD = 128
OWNED = 4
F32 = jnp.float32
BF16 = jnp.bfloat16
ROOMY, WHOLE = 24, 60
SM = pl.BlockSpec(memory_space=pltpu.SMEM)
ANY = pl.BlockSpec(memory_space=pl.ANY)


VM = pl.BlockSpec(memory_space=pltpu.VMEM)


def params(limit):
    return pltpu.CompilerParams(vmem_limit_bytes=limit * 2**20)


def cost(flops, arrays, weight=1):
    moved = sum(math.prod(x.shape) * x.dtype.itemsize for x in arrays)
    return pl.CostEstimate(flops=flops * weight, bytes_accessed=moved * weight, transcendentals=0)


def call(body, scalars, ins, raws, outs, flops, scratch=(), after=()):
    used = len(scalars) + len(ins) + len(raws)

    def kernel(*refs):
        body(*refs[:used], *refs[used + len(after) :])

    return pl.pallas_call(
        kernel,
        out_shape=tuple(outs),
        in_specs=[SM] * len(scalars) + [VM] * len(ins) + [ANY] * (len(raws) + len(after)),
        out_specs=tuple([VM] * len(outs)),
        scratch_shapes=list(scratch),
        compiler_params=params(ROOMY),
        cost_estimate=cost(flops, list(ins) + list(raws) + list(outs)),
    )(*scalars, *ins, *raws, *after)


def sds(shape, dtype=BF16):
    return jax.ShapeDtypeStruct(shape, dtype)


def block(number, width):
    return pl.ds(pl.multiple_of(number * width, width), width)


def interleave(first, second):
    n, f = first.shape
    a, b = first.reshape(n // 8, 8, f), second.reshape(n // 8, 8, f)
    low = lax.broadcasted_iota(jnp.int32, a.shape, 1) < OWNED
    t0 = jnp.where(low, a, pltpu.roll(b, OWNED, 1))
    t1 = jnp.where(low, pltpu.roll(a, OWNED, 1), b)
    return t0.reshape(n, f), t1.reshape(n, f)


def deinterleave(t0, t1):
    n, f = t0.shape
    t0, t1 = t0.reshape(n // 8, 8, f), t1.reshape(n // 8, 8, f)
    low = lax.broadcasted_iota(jnp.int32, t0.shape, 1) < OWNED
    a = jnp.where(low, t0, pltpu.roll(t1, OWNED, 1))
    b = jnp.where(low, pltpu.roll(t0, OWNED, 1), t1)
    return a.reshape(n, f), b.reshape(n, f)


def fetch(sources, targets, sems):
    copies = [pltpu.make_async_copy(s, t, sems.at[i]) for i, (s, t) in enumerate(zip(sources, targets))]
    for copy in copies:
        copy.start()
    return copies


def lanes(t, head, wide):
    return slice(t * wide + head * HD, t * wide + (head + 1) * HD)


def attend(q_ref, q_at, keys, vals, start, bits, out_ref, out_at):
    n = q_ref.shape[0]
    tile = min(256, n)
    factor = math.log2(math.e) / HD**0.5
    for i in range(n // tile):
        q = q_ref[i * tile : (i + 1) * tile, q_at]
        scores = []
        upto = start + (i + 1) * tile
        used = []
        base = 0
        for k_ref, k_at in keys:
            have = k_ref.shape[0]
            take = min(have, upto - base)
            used.append((base, take))
            s = lax.dot_general(q, k_ref[:take, k_at], (((1,), (1,)), ((), ())), preferred_element_type=F32)
            ta = lax.broadcasted_iota(jnp.int32, s.shape, 0) + (start + i * tile)
            tb = lax.broadcasted_iota(jnp.int32, s.shape, 1) + base
            ok = (((ta ^ tb) & bits) == 0) & (tb <= ta)
            scores.append(jnp.where(ok, s * factor, -jnp.inf))
            base += have
        top = scores[0].max(axis=-1, keepdims=True)
        for s in scores[1:]:
            top = jnp.maximum(top, s.max(axis=-1, keepdims=True))
        expo = [jnp.exp2(s - top) for s in scores]
        total = sum(e.sum(axis=-1, keepdims=True) for e in expo)
        out = 0.0
        for e, (v_ref, v_at), (_, take) in zip(expo, vals, used):
            out = out + jnp.dot(e.astype(BF16), v_ref[:take, v_at], preferred_element_type=F32)
        out_ref[i * tile : (i + 1) * tile, out_at] = (out / total).astype(BF16)


def permute_kernel(samples_hbm, out0_hbm, out1_hbm, in_ref, out_ref, sems):
    cols = samples_hbm.shape[1]
    step = cols // 4
    spans = [pl.ds(i * step, step) for i in range(4)]
    arriving = fetch([samples_hbm.at[:, at] for at in spans], [in_ref.at[:, at] for at in spans], sems.at[0])
    leaving = []
    for i, at in enumerate(spans):
        arriving[i].wait()
        halves = interleave(in_ref[0, at, :].astype(F32), in_ref[1, at, :].astype(F32))
        for k, half in enumerate(halves):
            out_ref[k, at, :] = half.astype(BF16)
        leaving += fetch([out_ref.at[k, at] for k in range(2)], [o.at[at] for o in (out0_hbm, out1_hbm)], sems.at[1 + i])
    for copy in leaving:
        copy.wait()


def permute(samples):
    outs = (sds(samples.shape[1:]),) * 2
    return pl.pallas_call(
        permute_kernel,
        out_shape=outs,
        in_specs=[ANY],
        out_specs=(ANY, ANY),
        scratch_shapes=[
            pltpu.VMEM(samples.shape, BF16),
            pltpu.VMEM(samples.shape, BF16),
            pltpu.SemaphoreType.DMA((5, 4)),
        ],
        compiler_params=params(WHOLE),
        cost_estimate=cost(samples.size, [samples, *outs]),
    )(samples)


def norm_project(h, refs, gain_ref, w_ref, copies, qkv_ref, sum_ref=None):
    width = refs[0].shape[1]
    features = 4 * width
    wide = w_ref.shape[2]
    total = jnp.sum(sum(ref[...].astype(F32) for ref in refs[sum_ref is not None :]), axis=-1, keepdims=True)
    if sum_ref is not None:
        total = total + jnp.sum(sum_ref[...], axis=-1, keepdims=True)
    mean = total * (1.0 / features)
    squares = 0.0
    for ref in refs:
        centred = ref[...].astype(F32) - mean
        squares = squares + centred * centred
    var = jnp.sum(squares, axis=-1, keepdims=True) * (1.0 / features)
    scale = lax.rsqrt(var + 1e-05)
    blocks = [block(h ^ flip, width) for flip in (0, 2, 1, 3)]
    normed = [
        ((ref[...].astype(F32) - mean) * scale * gain_ref[:, where]).astype(BF16)
        for ref, where in zip(refs, blocks)
    ]
    for copy in copies:
        copy.wait()
    for t in range(3):
        product = sum(
            jnp.dot(x, w_ref[t, where, :], preferred_element_type=F32) for x, where in zip(normed, blocks)
        )
        qkv_ref[:, t * wide : (t + 1) * wide] = product.astype(BF16)


def heads(qkv_ref, bits, attn_ref):
    wide = attn_ref.shape[1]
    for head in range(wide // HD):
        keys, vals = lanes(1, head, wide), lanes(2, head, wide)
        attend(qkv_ref, lanes(0, head, wide), [(qkv_ref, keys)], [(qkv_ref, vals)], 0, bits, attn_ref, lanes(0, head, wide))


def sum_kernel(x_ref, sum_ref):
    lanes = sum_ref.shape[1]
    sum_ref[...] = sum(x_ref[:, i : i + lanes].astype(F32) for i in range(0, x_ref.shape[1], lanes))


def col_kernel(n_sums, h_ref, a, b, c, d, gain_ref, w_ref, *refs):
    attn_ref, qkv_ref = refs[-2:]
    norm_project(h_ref[0], (a, b, c, d), gain_ref, w_ref, (), qkv_ref, refs[0] if n_sums else None)
    heads(qkv_ref, OWNED - 1, attn_ref)


def row_kernel(h_ref, *refs):
    parts_hbm, gain_hbm, w_hbm = refs[:4], refs[4], refs[5]
    x_ref, held_ref, gain_ref, w_ref, qkv_ref, sems = refs[-6:]
    outs_hbm = refs[-8:-6]
    first = fetch([gain_hbm] + [p.at[0] for p in parts_hbm], [gain_ref] + [x_ref.at[0, i] for i in range(4)], sems)
    weights = fetch([w_hbm], [w_ref], sems.at[5:])
    second = fetch([p.at[1] for p in parts_hbm], [x_ref.at[1, i] for i in range(4)], sems.at[6:])
    for row, ready, copies in ((0, first, weights), (1, second, ())):
        for copy in ready:
            copy.wait()
        norm_project(h_ref[0], [x_ref.at[row, i] for i in range(4)], gain_ref, w_ref, copies, qkv_ref)
        heads(qkv_ref, 0, held_ref.at[row])
    halves = interleave(held_ref[0].astype(F32), held_ref[1].astype(F32))
    leaving = []
    for i, half in enumerate(halves):
        held_ref[2 + i] = half.astype(BF16)
        leaving += fetch([held_ref.at[2 + i]], [outs_hbm[i]], sems.at[i:])
    for copy in leaving:
        copy.wait()


def out_dot(row_ref, col_ref, wr_ref, wc_ref, where):
    return jnp.dot(row_ref[...], wr_ref[:, where], preferred_element_type=F32) + jnp.dot(
        col_ref[...], wc_ref[:, where], preferred_element_type=F32
    )


def out_core_kernel(h_ref, row_ref, col_ref, wr_ref, wc_ref, y3_ref, y1_ref):
    h = h_ref[0]
    width = y3_ref.shape[1]
    y3_ref[...] = out_dot(row_ref, col_ref, wr_ref, wc_ref, block(h ^ 3, width)).astype(BF16)
    y1_ref[...] = out_dot(row_ref, col_ref, wr_ref, wc_ref, block(h ^ 1, width)).astype(BF16)


def out_chip_kernel(h_ref, row_ref, col_ref, wr_ref, wc_ref, r2_ref, s2_ref):
    width = s2_ref.shape[1]
    own = out_dot(row_ref, col_ref, wr_ref, wc_ref, block(h_ref[0] ^ 2, width))
    s2_ref[...] = (own + r2_ref[...].astype(F32)).astype(BF16)


def out_own_kernel(h_ref, row_ref, col_ref, wr_ref, wc_ref, r0_ref, own_ref):
    width = own_ref.shape[1]
    own = out_dot(row_ref, col_ref, wr_ref, wc_ref, block(h_ref[0], width))
    own_ref[...] = own + r0_ref[...].astype(F32)


def final_kernel(samples_ref, own0_ref, rx0_ref, own1_ref, rx1_ref, out_ref):
    cols = samples_ref.shape[1]
    step = min(64, cols)

    @pl.loop(0, cols // step)
    def _(i):
        at = pl.ds(pl.multiple_of(i * step, step), step)
        pair = deinterleave(
            own0_ref[at, :] + rx0_ref[at, :].astype(F32), own1_ref[at, :] + rx1_ref[at, :].astype(F32)
        )
        for r in range(2):
            out_ref[r, at, :] = (samples_ref[r, at, :].astype(F32) + pair[r]).astype(BF16)


def shards(samples, norm_gain, row_qkv, col_qkv, row_out, col_out):
    rows, cols, width = samples.shape
    assert rows == 2
    wide = col_qkv.shape[2]
    features = 4 * width
    tokens = cols
    h = lax.axis_index("head").astype(jnp.int32).reshape(1)
    gain = norm_gain.reshape(1, features)
    dma = pltpu.SemaphoreType.DMA

    def over_chip(x):
        return lax.ppermute(x, "head", [(i, i ^ 2) for i in range(4)])

    def over_core(x):
        return lax.ppermute(x, "head", [(i, i ^ 1) for i in range(4)])

    def exchange(x):
        return lax.all_to_all(x, "row", 0, 0, tiled=True)

    def gather(a):
        b = over_chip(a)
        return a, b, over_core(a), over_core(b)

    flops = 2 * tokens * features * 3 * wide + 4 * tokens * tokens * wide

    def cols(parts, after, sums=()):
        return call(
            functools.partial(col_kernel, len(sums)),
            (h,),
            (*parts, gain, col_qkv, *sums),
            (),
            (sds((tokens, wide)),),
            flops,
            [pltpu.VMEM((tokens, 3 * wide), BF16)],
            after,
        )[0]

    def both_rows(parts, after, weight):
        outs = (sds((tokens, wide)),) * 2
        return pl.pallas_call(
            row_kernel,
            out_shape=outs,
            in_specs=[SM] + [ANY] * (6 + len(after)),
            out_specs=(ANY, ANY),
            scratch_shapes=[
                pltpu.VMEM((2, 4, tokens, width), BF16),
                pltpu.VMEM((4, tokens, wide), BF16),
                pltpu.VMEM(gain.shape, F32),
                pltpu.VMEM(row_qkv.shape, BF16),
                pltpu.VMEM((tokens, 3 * wide), BF16),
                dma((10,)),
            ],
            compiler_params=params(WHOLE),
            cost_estimate=cost(2 * flops, parts, weight),
        )(h, *parts, gain, row_qkv, *after)

    piece = 4 * tokens * wide * width

    def out(row_attn, col_attn, after, after_chip):
        ops = (row_attn, col_attn, row_out, col_out)
        y3, y1 = call(out_core_kernel, (h,), ops, (), (sds((tokens, width)),) * 2, 2 * piece, (), after)
        (s2,) = call(out_chip_kernel, (h,), ops + (over_core(y3),), (), (sds((tokens, width)),), piece, (), after_chip)

        def own(after):
            more = ops + (over_core(y1),)
            return call(out_own_kernel, (h,), more, (), (sds((tokens, width), F32),), piece, (), after)[0]

        return own, s2, over_chip(s2)

    every = gather(samples)
    mixed0, mixed1 = permute(samples)
    start0 = exchange(mixed0)
    chip0 = over_chip(start0)
    mixed1, start0 = lax.optimization_barrier((mixed1, start0))
    start1 = exchange(mixed1)
    rows0, rows1 = both_rows(every, (), 1)
    core0, diagonal0 = over_core(start0), over_core(chip0)
    start0, rows0 = lax.optimization_barrier((start0, rows0))
    attn0 = cols((start0, chip0, core0, diagonal0), ())
    start1, attn0, rows0 = lax.optimization_barrier((start1, attn0, rows0))
    chip1 = over_chip(start1)
    back0 = exchange(attn0)
    (sums,) = call(sum_kernel, (), (start1,), (), (sds((tokens, HD), F32),), 4 * flops)
    attn1 = cols((start1, chip1, over_core(start1), over_core(chip1)), (), (sums,))
    back1 = exchange(attn1)
    own0, s0, rx0 = out(rows0, back0, (attn1,), ())
    own1, s1, rx1 = out(rows1, back1, (rx0,), ())
    own0 = own0((s1,))
    own1 = own1((own0,))
    return call(final_kernel, (), (samples, own0, rx0, own1, rx1), (), (sds(samples.shape),), samples.size)[0]


def solution(mesh):
    placed = (
        P("row", None, "head"),
        P(),
        P(None, None, "head"),
        P(None, None, "head"),
        P("head", None),
        P("head", None),
    )
    return jax.shard_map(
        shards, mesh=mesh, in_specs=placed, out_specs=P("row", None, "head"), check_vma=False
    )
```

```python
import functools
import math

import jax
import jax.numpy as jnp
from jax import lax
from jax.experimental import pallas as pl
from jax.experimental.pallas import tpu as pltpu
from jax.sharding import PartitionSpec as P

HD = 128
OWNED = 4
F32 = jnp.float32
BF16 = jnp.bfloat16
ROOMY, WHOLE = 24, 60
SM = pl.BlockSpec(memory_space=pltpu.SMEM)
ANY = pl.BlockSpec(memory_space=pl.ANY)


VM = pl.BlockSpec(memory_space=pltpu.VMEM)


def params(limit):
    return pltpu.CompilerParams(vmem_limit_bytes=limit * 2**20)


def cost(flops, arrays, weight=1):
    moved = sum(math.prod(x.shape) * x.dtype.itemsize for x in arrays)
    return pl.CostEstimate(flops=flops * weight, bytes_accessed=moved * weight, transcendentals=0)


def call(body, scalars, ins, raws, outs, flops, scratch=(), after=()):
    used = len(scalars) + len(ins) + len(raws)

    def kernel(*refs):
        body(*refs[:used], *refs[used + len(after) :])

    return pl.pallas_call(
        kernel,
        out_shape=tuple(outs),
        in_specs=[SM] * len(scalars) + [VM] * len(ins) + [ANY] * (len(raws) + len(after)),
        out_specs=tuple([VM] * len(outs)),
        scratch_shapes=list(scratch),
        compiler_params=params(ROOMY),
        cost_estimate=cost(flops, list(ins) + list(raws) + list(outs)),
    )(*scalars, *ins, *raws, *after)


def sds(shape, dtype=BF16):
    return jax.ShapeDtypeStruct(shape, dtype)


def block(number, width):
    return pl.ds(pl.multiple_of(number * width, width), width)


def interleave(first, second):
    n, f = first.shape
    a, b = first.reshape(n // 8, 8, f), second.reshape(n // 8, 8, f)
    low = lax.broadcasted_iota(jnp.int32, a.shape, 1) < OWNED
    t0 = jnp.where(low, a, pltpu.roll(b, OWNED, 1))
    t1 = jnp.where(low, pltpu.roll(a, OWNED, 1), b)
    return t0.reshape(n, f), t1.reshape(n, f)


def deinterleave(t0, t1):
    n, f = t0.shape
    t0, t1 = t0.reshape(n // 8, 8, f), t1.reshape(n // 8, 8, f)
    low = lax.broadcasted_iota(jnp.int32, t0.shape, 1) < OWNED
    a = jnp.where(low, t0, pltpu.roll(t1, OWNED, 1))
    b = jnp.where(low, pltpu.roll(t0, OWNED, 1), t1)
    return a.reshape(n, f), b.reshape(n, f)


def fetch(sources, targets, sems):
    copies = [pltpu.make_async_copy(s, t, sems.at[i]) for i, (s, t) in enumerate(zip(sources, targets))]
    for copy in copies:
        copy.start()
    return copies


def lanes(t, head, wide):
    return slice(t * wide + head * HD, t * wide + (head + 1) * HD)


def attend(q_ref, q_at, keys, vals, start, bits, out_ref, out_at):
    n = q_ref.shape[0]
    tile = min(256, n)
    factor = math.log2(math.e) / HD**0.5
    for i in range(n // tile):
        q = q_ref[i * tile : (i + 1) * tile, q_at]
        scores = []
        upto = start + (i + 1) * tile
        used = []
        base = 0
        for k_ref, k_at in keys:
            have = k_ref.shape[0]
            take = min(have, upto - base)
            used.append((base, take))
            s = lax.dot_general(q, k_ref[:take, k_at], (((1,), (1,)), ((), ())), preferred_element_type=F32)
            ta = lax.broadcasted_iota(jnp.int32, s.shape, 0) + (start + i * tile)
            tb = lax.broadcasted_iota(jnp.int32, s.shape, 1) + base
            ok = (((ta ^ tb) & bits) == 0) & (tb <= ta)
            scores.append(jnp.where(ok, s * factor, -jnp.inf))
            base += have
        top = scores[0].max(axis=-1, keepdims=True)
        for s in scores[1:]:
            top = jnp.maximum(top, s.max(axis=-1, keepdims=True))
        expo = [jnp.exp2(s - top) for s in scores]
        total = sum(e.sum(axis=-1, keepdims=True) for e in expo)
        out = 0.0
        for e, (v_ref, v_at), (_, take) in zip(expo, vals, used):
            out = out + jnp.dot(e.astype(BF16), v_ref[:take, v_at], preferred_element_type=F32)
        out_ref[i * tile : (i + 1) * tile, out_at] = (out / total).astype(BF16)


def permute_kernel(samples_hbm, out0_hbm, out1_hbm, row0_hbm, row1_hbm, in_ref, out_ref, sems):
    cols = samples_hbm.shape[1]
    step = cols // 4
    spans = [pl.ds(i * step, step) for i in range(4)]
    arriving = fetch([samples_hbm.at[:, at] for at in spans], [in_ref.at[:, at] for at in spans], sems.at[0])
    leaving = []
    for i, at in enumerate(spans):
        arriving[i].wait()
        leaving += fetch([in_ref.at[r, at] for r in range(2)], [o.at[at] for o in (row0_hbm, row1_hbm)], sems.at[5 + i])
        halves = interleave(in_ref[0, at, :].astype(F32), in_ref[1, at, :].astype(F32))
        for k, half in enumerate(halves):
            out_ref[k, at, :] = half.astype(BF16)
        leaving += fetch([out_ref.at[k, at] for k in range(2)], [o.at[at] for o in (out0_hbm, out1_hbm)], sems.at[1 + i])
    for copy in leaving:
        copy.wait()


def permute(samples):
    outs = (sds(samples.shape[1:]),) * 4
    return pl.pallas_call(
        permute_kernel,
        out_shape=outs,
        in_specs=[ANY],
        out_specs=(ANY,) * 4,
        scratch_shapes=[
            pltpu.VMEM(samples.shape, BF16),
            pltpu.VMEM(samples.shape, BF16),
            pltpu.SemaphoreType.DMA((9, 4)),
        ],
        compiler_params=params(WHOLE),
        cost_estimate=cost(samples.size, [samples, *outs]),
    )(samples)


def norm_project(h, refs, gain_ref, w_ref, copies, qkv_ref, sum_ref=None):
    width = refs[0].shape[1]
    features = 4 * width
    wide = w_ref.shape[2]
    total = jnp.sum(sum(ref[...].astype(F32) for ref in refs[sum_ref is not None :]), axis=-1, keepdims=True)
    if sum_ref is not None:
        total = total + jnp.sum(sum_ref[...], axis=-1, keepdims=True)
    mean = total * (1.0 / features)
    squares = 0.0
    for ref in refs:
        centred = ref[...].astype(F32) - mean
        squares = squares + centred * centred
    var = jnp.sum(squares, axis=-1, keepdims=True) * (1.0 / features)
    scale = lax.rsqrt(var + 1e-05)
    blocks = [block(h ^ flip, width) for flip in (0, 2, 1, 3)]
    normed = [
        ((ref[...].astype(F32) - mean) * scale * gain_ref[:, where]).astype(BF16)
        for ref, where in zip(refs, blocks)
    ]
    for copy in copies:
        copy.wait()
    for t in range(3):
        product = sum(
            jnp.dot(x, w_ref[t, where, :], preferred_element_type=F32) for x, where in zip(normed, blocks)
        )
        qkv_ref[:, t * wide : (t + 1) * wide] = product.astype(BF16)


def heads(qkv_ref, bits, attn_ref):
    wide = attn_ref.shape[1]
    for head in range(wide // HD):
        keys, vals = lanes(1, head, wide), lanes(2, head, wide)
        attend(qkv_ref, lanes(0, head, wide), [(qkv_ref, keys)], [(qkv_ref, vals)], 0, bits, attn_ref, lanes(0, head, wide))


def sum_kernel(x_ref, sum_ref):
    lanes = sum_ref.shape[1]
    sum_ref[...] = sum(x_ref[:, i : i + lanes].astype(F32) for i in range(0, x_ref.shape[1], lanes))


def col_kernel(n_sums, h_ref, a, b, c, d, gain_ref, w_ref, *refs):
    attn_ref, qkv_ref = refs[-2:]
    norm_project(h_ref[0], (a, b, c, d), gain_ref, w_ref, (), qkv_ref, refs[0] if n_sums else None)
    heads(qkv_ref, OWNED - 1, attn_ref)


def row_kernel(row, n_more, h_ref, *refs):
    parts_hbm, more_hbm, (gain_hbm, w_hbm) = refs[:4], refs[4 : 4 + n_more], refs[4 + n_more : 6 + n_more]
    n_out = 2 if n_more else 1
    x_ref, held_ref, gain_ref, w_ref, qkv_ref, sems, more_sems = refs[-7:]
    outs_hbm = refs[-7 - n_out : -7]
    ready = fetch([gain_hbm, parts_hbm[0].at[row], *parts_hbm[1:]], [gain_ref] + [x_ref.at[i] for i in range(4)], sems)
    copies = fetch([w_hbm], [w_ref], sems.at[5:])
    earlier = fetch(more_hbm, [held_ref.at[0]], more_sems)
    for copy in ready:
        copy.wait()
    norm_project(h_ref[0], [x_ref.at[i] for i in range(4)], gain_ref, w_ref, copies, qkv_ref)
    heads(qkv_ref, 0, held_ref.at[n_more])
    if n_more:
        earlier[0].wait()
        halves = interleave(held_ref[0].astype(F32), held_ref[1].astype(F32))
        for i, half in enumerate(halves):
            held_ref[i] = half.astype(BF16)
    for copy in fetch([held_ref.at[i] for i in range(n_out)], outs_hbm, more_sems):
        copy.wait()


def out_dot(row_ref, col_ref, wr_ref, wc_ref, where):
    return jnp.dot(row_ref[...], wr_ref[:, where], preferred_element_type=F32) + jnp.dot(
        col_ref[...], wc_ref[:, where], preferred_element_type=F32
    )


def out_core_kernel(h_ref, row_ref, col_ref, wr_ref, wc_ref, y3_ref, y1_ref):
    h = h_ref[0]
    width = y3_ref.shape[1]
    y3_ref[...] = out_dot(row_ref, col_ref, wr_ref, wc_ref, block(h ^ 3, width)).astype(BF16)
    y1_ref[...] = out_dot(row_ref, col_ref, wr_ref, wc_ref, block(h ^ 1, width)).astype(BF16)


def out_chip_kernel(h_ref, row_ref, col_ref, wr_ref, wc_ref, r2_ref, s2_ref):
    width = s2_ref.shape[1]
    own = out_dot(row_ref, col_ref, wr_ref, wc_ref, block(h_ref[0] ^ 2, width))
    s2_ref[...] = (own + r2_ref[...].astype(F32)).astype(BF16)


def out_own_kernel(h_ref, row_ref, col_ref, wr_ref, wc_ref, r0_ref, own_ref):
    width = own_ref.shape[1]
    own = out_dot(row_ref, col_ref, wr_ref, wc_ref, block(h_ref[0], width))
    own_ref[...] = own + r0_ref[...].astype(F32)


def final_kernel(samples_ref, own0_ref, rx0_ref, own1_ref, rx1_ref, out_hbm, out_ref, sems):
    pieces = sems.shape[0]
    step = samples_ref.shape[1] // pieces
    leaving = []
    for i in range(pieces):
        at = slice(i * step, (i + 1) * step)
        pair = deinterleave(
            own0_ref[at, :] + rx0_ref[at, :].astype(F32), own1_ref[at, :] + rx1_ref[at, :].astype(F32)
        )
        for r in range(2):
            out_ref[r, at, :] = (samples_ref[r, at, :].astype(F32) + pair[r]).astype(BF16)
        leaving += fetch([out_ref.at[:, at]], [out_hbm.at[:, at]], sems.at[i:])
    for copy in leaving:
        copy.wait()


def final(*ins):
    samples = ins[0]
    pieces = min(8, samples.shape[1] // 16)
    return pl.pallas_call(
        final_kernel,
        out_shape=sds(samples.shape),
        in_specs=[VM] * len(ins),
        out_specs=ANY,
        scratch_shapes=[pltpu.VMEM(samples.shape, BF16), pltpu.SemaphoreType.DMA((pieces,))],
        compiler_params=params(ROOMY),
        cost_estimate=cost(samples.size, [*ins, samples]),
    )(*ins)


def shards(samples, norm_gain, row_qkv, col_qkv, row_out, col_out):
    rows, cols, width = samples.shape
    assert rows == 2
    wide = col_qkv.shape[2]
    features = 4 * width
    tokens = cols
    h = lax.axis_index("head").astype(jnp.int32).reshape(1)
    gain = norm_gain.reshape(1, features)
    dma = pltpu.SemaphoreType.DMA

    def over_chip(x):
        return lax.ppermute(x, "head", [(i, i ^ 2) for i in range(4)])

    def over_core(x):
        return lax.ppermute(x, "head", [(i, i ^ 1) for i in range(4)])

    def exchange(x):
        return lax.all_to_all(x, "row", 0, 0, tiled=True)

    def gather(a):
        b = over_chip(a)
        return a, b, over_core(a), over_core(b)

    flops = 2 * tokens * features * 3 * wide + 4 * tokens * tokens * wide

    def cols(parts, after, sums=()):
        return call(
            functools.partial(col_kernel, len(sums)),
            (h,),
            (*parts, gain, col_qkv, *sums),
            (),
            (sds((tokens, wide)),),
            flops,
            [pltpu.VMEM((tokens, 3 * wide), BF16)],
            after,
        )[0]

    def row(r, parts, more, after, weight):
        outs = tuple([sds((tokens, wide))] * (1 + len(more)))
        return pl.pallas_call(
            functools.partial(row_kernel, r, len(more)),
            out_shape=outs,
            in_specs=[SM] + [ANY] * (6 + len(more) + len(after)),
            out_specs=tuple([ANY] * len(outs)),
            scratch_shapes=[
                pltpu.VMEM((4, tokens, width), BF16),
                pltpu.VMEM((2, tokens, wide), BF16),
                pltpu.VMEM(gain.shape, F32),
                pltpu.VMEM(row_qkv.shape, BF16),
                pltpu.VMEM((tokens, 3 * wide), BF16),
                dma((6,)),
                dma((2,)),
            ],
            compiler_params=params(WHOLE),
            cost_estimate=cost(flops, parts, weight),
        )(h, *parts, *more, gain, row_qkv, *after)

    piece = 4 * tokens * wide * width

    def out(row_attn, col_attn, after, after_chip):
        ops = (row_attn, col_attn, row_out, col_out)
        y3, y1 = call(out_core_kernel, (h,), ops, (), (sds((tokens, width)),) * 2, 2 * piece, (), after)
        (s2,) = call(out_chip_kernel, (h,), ops + (over_core(y3),), (), (sds((tokens, width)),), piece, (), after_chip)

        def own(after):
            more = ops + (over_core(y1),)
            return call(out_own_kernel, (h,), more, (), (sds((tokens, width), F32),), piece, (), after)[0]

        return own, s2, over_chip(s2)

    mixed0, mixed1, first, second = permute(samples)
    start0 = exchange(mixed0)
    parts = gather(first)
    (row0,) = row(0, (samples, *parts[1:]), (), (), 1)
    second, _ = lax.optimization_barrier((second, parts[1]))
    parts = gather(second)
    start0, row0 = lax.optimization_barrier((start0, row0))
    chip0 = over_chip(start0)
    mixed1, start0 = lax.optimization_barrier((mixed1, start0))
    start1 = exchange(mixed1)
    rows0, rows1 = row(1, (samples, *parts[1:]), (row0,), (), 1)
    core0, diagonal0 = over_core(start0), over_core(chip0)
    start0, rows0 = lax.optimization_barrier((start0, rows0))
    attn0 = cols((start0, chip0, core0, diagonal0), ())
    start1, attn0, rows0 = lax.optimization_barrier((start1, attn0, rows0))
    chip1 = over_chip(start1)
    back0 = exchange(attn0)
    (sums,) = call(sum_kernel, (), (start1,), (), (sds((tokens, HD), F32),), 4 * flops)
    attn1 = cols((start1, chip1, over_core(start1), over_core(chip1)), (), (sums,))
    back1 = exchange(attn1)
    own0, s0, rx0 = out(rows0, back0, (attn1,), ())
    own1, s1, rx1 = out(rows1, back1, (rx0,), ())
    own0 = own0((s1,))
    own1 = own1((own0,))
    return final(samples, own0, rx0, own1, rx1)


def solution(mesh):
    placed = (
        P("row", None, "head"),
        P(),
        P(None, None, "head"),
        P(None, None, "head"),
        P("head", None),
        P("head", None),
    )
    return jax.shard_map(
        shards, mesh=mesh, in_specs=placed, out_specs=P("row", None, "head"), check_vma=False
    )
```

```python
import functools
import math

import jax
import jax.numpy as jnp
from jax import lax
from jax.experimental import pallas as pl
from jax.experimental.pallas import tpu as pltpu
from jax.sharding import PartitionSpec as P

HD = 128
OWNED = 4
F32 = jnp.float32
BF16 = jnp.bfloat16
ROOMY, WHOLE = 24, 60
SM = pl.BlockSpec(memory_space=pltpu.SMEM)
ANY = pl.BlockSpec(memory_space=pl.ANY)


VM = pl.BlockSpec(memory_space=pltpu.VMEM)


def params(limit):
    return pltpu.CompilerParams(vmem_limit_bytes=limit * 2**20)


def cost(flops, arrays, weight=1):
    moved = sum(math.prod(x.shape) * x.dtype.itemsize for x in arrays)
    return pl.CostEstimate(flops=flops * weight, bytes_accessed=moved * weight, transcendentals=0)


def call(body, scalars, ins, raws, outs, flops, scratch=(), after=()):
    used = len(scalars) + len(ins) + len(raws)

    def kernel(*refs):
        body(*refs[:used], *refs[used + len(after) :])

    return pl.pallas_call(
        kernel,
        out_shape=tuple(outs),
        in_specs=[SM] * len(scalars) + [VM] * len(ins) + [ANY] * (len(raws) + len(after)),
        out_specs=tuple([VM] * len(outs)),
        scratch_shapes=list(scratch),
        compiler_params=params(ROOMY),
        cost_estimate=cost(flops, list(ins) + list(raws) + list(outs)),
    )(*scalars, *ins, *raws, *after)


def sds(shape, dtype=BF16):
    return jax.ShapeDtypeStruct(shape, dtype)


def block(number, width):
    return pl.ds(pl.multiple_of(number * width, width), width)


def interleave(first, second):
    n, f = first.shape
    a, b = first.reshape(n // 8, 8, f), second.reshape(n // 8, 8, f)
    low = lax.broadcasted_iota(jnp.int32, a.shape, 1) < OWNED
    t0 = jnp.where(low, a, pltpu.roll(b, OWNED, 1))
    t1 = jnp.where(low, pltpu.roll(a, OWNED, 1), b)
    return t0.reshape(n, f), t1.reshape(n, f)


def deinterleave(t0, t1):
    n, f = t0.shape
    t0, t1 = t0.reshape(n // 8, 8, f), t1.reshape(n // 8, 8, f)
    low = lax.broadcasted_iota(jnp.int32, t0.shape, 1) < OWNED
    a = jnp.where(low, t0, pltpu.roll(t1, OWNED, 1))
    b = jnp.where(low, pltpu.roll(t0, OWNED, 1), t1)
    return a.reshape(n, f), b.reshape(n, f)


def fetch(sources, targets, sems):
    copies = [pltpu.make_async_copy(s, t, sems.at[i]) for i, (s, t) in enumerate(zip(sources, targets))]
    for copy in copies:
        copy.start()
    return copies


def lanes(t, head, wide):
    return slice(t * wide + head * HD, t * wide + (head + 1) * HD)


def attend(q_ref, q_at, keys, vals, start, bits, out_ref, out_at):
    n = q_ref.shape[0]
    tile = min(256, n)
    factor = math.log2(math.e) / HD**0.5
    for i in range(n // tile):
        q = q_ref[i * tile : (i + 1) * tile, q_at]
        scores = []
        upto = start + (i + 1) * tile
        used = []
        base = 0
        for k_ref, k_at in keys:
            have = k_ref.shape[0]
            take = min(have, upto - base)
            used.append((base, take))
            s = lax.dot_general(q, k_ref[:take, k_at], (((1,), (1,)), ((), ())), preferred_element_type=F32)
            ta = lax.broadcasted_iota(jnp.int32, s.shape, 0) + (start + i * tile)
            tb = lax.broadcasted_iota(jnp.int32, s.shape, 1) + base
            ok = (((ta ^ tb) & bits) == 0) & (tb <= ta)
            scores.append(jnp.where(ok, s * factor, -jnp.inf))
            base += have
        top = scores[0].max(axis=-1, keepdims=True)
        for s in scores[1:]:
            top = jnp.maximum(top, s.max(axis=-1, keepdims=True))
        expo = [jnp.exp2(s - top) for s in scores]
        total = sum(e.sum(axis=-1, keepdims=True) for e in expo)
        out = 0.0
        for e, (v_ref, v_at), (_, take) in zip(expo, vals, used):
            out = out + jnp.dot(e.astype(BF16), v_ref[:take, v_at], preferred_element_type=F32)
        out_ref[i * tile : (i + 1) * tile, out_at] = (out / total).astype(BF16)


def permute_kernel(samples_hbm, out0_hbm, out1_hbm, row0_hbm, row1_hbm, in_ref, out_ref, sems):
    cols = samples_hbm.shape[1]
    step = cols // 4
    spans = [pl.ds(i * step, step) for i in range(4)]
    arriving = fetch([samples_hbm.at[:, at] for at in spans], [in_ref.at[:, at] for at in spans], sems.at[0])
    leaving = []
    for i, at in enumerate(spans):
        arriving[i].wait()
        leaving += fetch([in_ref.at[r, at] for r in range(2)], [o.at[at] for o in (row0_hbm, row1_hbm)], sems.at[5 + i])
        halves = interleave(in_ref[0, at, :].astype(F32), in_ref[1, at, :].astype(F32))
        for k, half in enumerate(halves):
            out_ref[k, at, :] = half.astype(BF16)
        leaving += fetch([out_ref.at[k, at] for k in range(2)], [o.at[at] for o in (out0_hbm, out1_hbm)], sems.at[1 + i])
    for copy in leaving:
        copy.wait()


def permute(samples):
    outs = (sds(samples.shape[1:]),) * 4
    return pl.pallas_call(
        permute_kernel,
        out_shape=outs,
        in_specs=[ANY],
        out_specs=(ANY,) * 4,
        scratch_shapes=[
            pltpu.VMEM(samples.shape, BF16),
            pltpu.VMEM(samples.shape, BF16),
            pltpu.SemaphoreType.DMA((9, 4)),
        ],
        compiler_params=params(WHOLE),
        cost_estimate=cost(samples.size, [samples, *outs]),
    )(samples)


def norm_project(h, refs, gain_ref, w_ref, copies, qkv_ref, sum_ref=None):
    width = refs[0].shape[1]
    features = 4 * width
    wide = w_ref.shape[2]
    total = jnp.sum(sum(ref[...].astype(F32) for ref in refs[sum_ref is not None :]), axis=-1, keepdims=True)
    if sum_ref is not None:
        total = total + jnp.sum(sum_ref[...], axis=-1, keepdims=True)
    mean = total * (1.0 / features)
    squares = 0.0
    for ref in refs:
        centred = ref[...].astype(F32) - mean
        squares = squares + centred * centred
    var = jnp.sum(squares, axis=-1, keepdims=True) * (1.0 / features)
    scale = lax.rsqrt(var + 1e-05)
    blocks = [block(h ^ flip, width) for flip in (0, 2, 1, 3)]
    normed = [
        ((ref[...].astype(F32) - mean) * scale * gain_ref[:, where]).astype(BF16)
        for ref, where in zip(refs, blocks)
    ]
    for copy in copies:
        copy.wait()
    for t in range(3):
        product = sum(
            jnp.dot(x, w_ref[t, where, :], preferred_element_type=F32) for x, where in zip(normed, blocks)
        )
        qkv_ref[:, t * wide : (t + 1) * wide] = product.astype(BF16)


def heads(qkv_ref, bits, attn_ref):
    wide = attn_ref.shape[1]
    for head in range(wide // HD):
        keys, vals = lanes(1, head, wide), lanes(2, head, wide)
        attend(qkv_ref, lanes(0, head, wide), [(qkv_ref, keys)], [(qkv_ref, vals)], 0, bits, attn_ref, lanes(0, head, wide))


def sum_kernel(x_ref, sum_ref):
    lanes = sum_ref.shape[1]
    sum_ref[...] = sum(x_ref[:, i : i + lanes].astype(F32) for i in range(0, x_ref.shape[1], lanes))


def col_kernel(n_sums, h_ref, a, b, c, d, gain_ref, w_ref, *refs):
    attn_ref, qkv_ref = refs[-2:]
    norm_project(h_ref[0], (a, b, c, d), gain_ref, w_ref, (), qkv_ref, refs[0] if n_sums else None)
    heads(qkv_ref, OWNED - 1, attn_ref)


def row_kernel(row, n_more, h_ref, *refs):
    parts_hbm, more_hbm, (gain_hbm, w_hbm) = refs[:4], refs[4 : 4 + n_more], refs[4 + n_more : 6 + n_more]
    n_out = 2 if n_more else 1
    x_ref, held_ref, gain_ref, w_ref, qkv_ref, sems, more_sems = refs[-7:]
    outs_hbm = refs[-7 - n_out : -7]
    ready = fetch([gain_hbm, parts_hbm[0].at[row], *parts_hbm[1:]], [gain_ref] + [x_ref.at[i] for i in range(4)], sems)
    copies = fetch([w_hbm], [w_ref], sems.at[5:])
    earlier = fetch(more_hbm, [held_ref.at[0]], more_sems)
    for copy in ready:
        copy.wait()
    norm_project(h_ref[0], [x_ref.at[i] for i in range(4)], gain_ref, w_ref, copies, qkv_ref)
    heads(qkv_ref, 0, held_ref.at[n_more])
    if n_more:
        earlier[0].wait()
        halves = interleave(held_ref[0].astype(F32), held_ref[1].astype(F32))
        for i, half in enumerate(halves):
            held_ref[i] = half.astype(BF16)
    for copy in fetch([held_ref.at[i] for i in range(n_out)], outs_hbm, more_sems):
        copy.wait()


def out_dot(row_ref, col_ref, wr_ref, wc_ref, where):
    return jnp.dot(row_ref[...], wr_ref[:, where], preferred_element_type=F32) + jnp.dot(
        col_ref[...], wc_ref[:, where], preferred_element_type=F32
    )


def out_core_kernel(flip, h_ref, row_ref, col_ref, wr_ref, wc_ref, y_ref):
    where = block(h_ref[0] ^ flip, y_ref.shape[1])
    y_ref[...] = out_dot(row_ref, col_ref, wr_ref, wc_ref, where).astype(BF16)


def out_chip_kernel(h_ref, row_ref, col_ref, wr_ref, wc_ref, r2_ref, s2_ref):
    width = s2_ref.shape[1]
    own = out_dot(row_ref, col_ref, wr_ref, wc_ref, block(h_ref[0] ^ 2, width))
    s2_ref[...] = (own + r2_ref[...].astype(F32)).astype(BF16)


def out_own_kernel(h_ref, row_ref, col_ref, wr_ref, wc_ref, r0_ref, own_ref):
    width = own_ref.shape[1]
    own = out_dot(row_ref, col_ref, wr_ref, wc_ref, block(h_ref[0], width))
    own_ref[...] = own + r0_ref[...].astype(F32)


def final_kernel(samples_ref, own0_ref, rx0_ref, own1_ref, rx1_ref, out_hbm, out_ref, sems):
    pieces = sems.shape[0]
    step = samples_ref.shape[1] // pieces
    leaving = []
    for i in range(pieces):
        at = slice(i * step, (i + 1) * step)
        pair = deinterleave(
            own0_ref[at, :] + rx0_ref[at, :].astype(F32), own1_ref[at, :] + rx1_ref[at, :].astype(F32)
        )
        for r in range(2):
            out_ref[r, at, :] = (samples_ref[r, at, :].astype(F32) + pair[r]).astype(BF16)
        leaving += fetch([out_ref.at[:, at]], [out_hbm.at[:, at]], sems.at[i:])
    for copy in leaving:
        copy.wait()


def final(*ins):
    samples = ins[0]
    pieces = min(8, samples.shape[1] // 16)
    return pl.pallas_call(
        final_kernel,
        out_shape=sds(samples.shape),
        in_specs=[VM] * len(ins),
        out_specs=ANY,
        scratch_shapes=[pltpu.VMEM(samples.shape, BF16), pltpu.SemaphoreType.DMA((pieces,))],
        compiler_params=params(ROOMY),
        cost_estimate=cost(samples.size, [*ins, samples]),
    )(*ins)


def shards(samples, norm_gain, row_qkv, col_qkv, row_out, col_out):
    rows, cols, width = samples.shape
    assert rows == 2
    wide = col_qkv.shape[2]
    features = 4 * width
    tokens = cols
    h = lax.axis_index("head").astype(jnp.int32).reshape(1)
    gain = norm_gain.reshape(1, features)
    dma = pltpu.SemaphoreType.DMA

    def over_chip(x):
        return lax.ppermute(x, "head", [(i, i ^ 2) for i in range(4)])

    def over_core(x):
        return lax.ppermute(x, "head", [(i, i ^ 1) for i in range(4)])

    def exchange(x):
        return lax.all_to_all(x, "row", 0, 0, tiled=True)

    def gather(a):
        b = over_chip(a)
        return a, b, over_core(a), over_core(b)

    flops = 2 * tokens * features * 3 * wide + 4 * tokens * tokens * wide

    def cols(parts, after, sums=()):
        return call(
            functools.partial(col_kernel, len(sums)),
            (h,),
            (*parts, gain, col_qkv, *sums),
            (),
            (sds((tokens, wide)),),
            flops,
            [pltpu.VMEM((tokens, 3 * wide), BF16)],
            after,
        )[0]

    def row(r, parts, more, after, weight):
        outs = tuple([sds((tokens, wide))] * (1 + len(more)))
        return pl.pallas_call(
            functools.partial(row_kernel, r, len(more)),
            out_shape=outs,
            in_specs=[SM] + [ANY] * (6 + len(more) + len(after)),
            out_specs=tuple([ANY] * len(outs)),
            scratch_shapes=[
                pltpu.VMEM((4, tokens, width), BF16),
                pltpu.VMEM((2, tokens, wide), BF16),
                pltpu.VMEM(gain.shape, F32),
                pltpu.VMEM(row_qkv.shape, BF16),
                pltpu.VMEM((tokens, 3 * wide), BF16),
                dma((6,)),
                dma((2,)),
            ],
            compiler_params=params(WHOLE),
            cost_estimate=cost(flops, parts, weight),
        )(h, *parts, *more, gain, row_qkv, *after)

    piece = 4 * tokens * wide * width

    def out(row_attn, col_attn, after, after_chip):
        ops = (row_attn, col_attn, row_out, col_out)
        (y3,) = call(functools.partial(out_core_kernel, 3), (h,), ops, (), (sds((tokens, width)),), piece, (), after)
        (y1,) = call(functools.partial(out_core_kernel, 1), (h,), ops, (), (sds((tokens, width)),), piece, (), (y3,))
        (s2,) = call(out_chip_kernel, (h,), ops + (over_core(y3),), (), (sds((tokens, width)),), piece, (), after_chip)

        def own(after):
            more = ops + (over_core(y1),)
            return call(out_own_kernel, (h,), more, (), (sds((tokens, width), F32),), piece, (), after)[0]

        return own, s2, over_chip(s2)

    mixed0, mixed1, first, second = permute(samples)
    start0 = exchange(mixed0)
    parts = gather(first)
    (row0,) = row(0, (samples, *parts[1:]), (), (), 1)
    second, _ = lax.optimization_barrier((second, parts[1]))
    parts = gather(second)
    start0, row0 = lax.optimization_barrier((start0, row0))
    chip0 = over_chip(start0)
    mixed1, start0 = lax.optimization_barrier((mixed1, start0))
    start1 = exchange(mixed1)
    rows0, rows1 = row(1, (samples, *parts[1:]), (row0,), (), 1)
    core0, diagonal0 = over_core(start0), over_core(chip0)
    start0, rows0 = lax.optimization_barrier((start0, rows0))
    attn0 = cols((start0, chip0, core0, diagonal0), ())
    start1, attn0, rows0 = lax.optimization_barrier((start1, attn0, rows0))
    chip1 = over_chip(start1)
    back0 = exchange(attn0)
    (sums,) = call(sum_kernel, (), (start1,), (), (sds((tokens, HD), F32),), 4 * flops)
    attn1 = cols((start1, chip1, over_core(start1), over_core(chip1)), (), (sums,))
    back1 = exchange(attn1)
    own0, s0, rx0 = out(rows0, back0, (attn1,), ())
    own1, s1, rx1 = out(rows1, back1, (rx0,), ())
    own0 = own0((s1,))
    own1 = own1((own0,))
    return final(samples, own0, rx0, own1, rx1)


def solution(mesh):
    placed = (
        P("row", None, "head"),
        P(),
        P(None, None, "head"),
        P(None, None, "head"),
        P("head", None),
        P("head", None),
    )
    return jax.shard_map(
        shards, mesh=mesh, in_specs=placed, out_specs=P("row", None, "head"), check_vma=False
    )
```
